32 devices in a mesh: sys: 2 (over y), row: 4 (over z), col: 4 (over x, core).
Axes of the slice: x: 2, y: 2, z: 4, core: 2. Of those that a mesh axis runs over, the one named last changes fastest.
Arguments:
- blocks: bfloat16 [8, 4, 16, 128, 128], P(('sys', 'row'), 'col'), parts along dimension 0, may hold values from -0.8984375 to 0.8984375
- pairs: int32 [8, 4, 16, 16, 2], P(('sys', 'row'), 'col'), parts along dimension 0, may hold values from 0 to 63, as said below
- term_count: int32 [8, 4, 16], P(('sys', 'row'), 'col'), parts along dimension 0, may hold values from 1 to 16
Outputs:
- purified: bfloat16 [8, 4, 16, 128, 128], P(('sys', 'row'), 'col'), parts along dimension 0
The draws below stay inside these ranges and needn't reach their ends.
There are 2 independent parts, one for each index of `sys`. The reference program is written for one: setup_inputs(seed, part) draws one part's arguments, and reference() takes and returns one part's arrays. A program takes and returns all parts, laid end to end along the dimension named above; each array names one. Nothing has to cross between parts.
Inputs may be any that keep to these rules, and one draw needn't show every extreme that they name: pairs[..., 0] is below 64 and pairs[..., 1] is below 64. For each grid position (r, c) and each r', the entries pairs[r, c, :, :, 1] that lie in [r' * 16, (r' + 1) * 16) take at most 8 distinct values, all terms counted, active or not; some grid position reaches 8 for some r'.
All inputs are finite; a program needn't handle non-finite values.
Results may differ from the reference program's by a relative error of at most 0.0048.
Values may be sent and summed in bfloat16 or wider, within the bound.
No kernel may reach another device: no remote copies, remote signals or barrier semaphores. Data moves between devices by JAX's collectives and lax.ppermute only.
A program may use at most 128 MiB of HBM per device.

```python
import jax
import jax.numpy as jnp
from jax import lax

B = 128
SL = 16
TERMS = 16
CAP = 8
PROW = 4
PCOL = 4


def draw_pairs(key, part):
    key = jax.random.fold_in(key, 11)
    key_left, key_source, key_pick, key_order, key_spot = jax.random.split(key, 5)
    shape = (PROW, PCOL, SL, TERMS)
    left_index = jax.random.randint(key_left, shape, 0, PCOL * SL)
    total = PROW * PCOL * SL * TERMS
    spot = jax.random.randint(key_spot, (), 0, total)
    position = jnp.arange(total, dtype=jnp.int32).reshape(shape)
    left_index = jnp.where(position == spot, PCOL * SL - 1, left_index)
    scores = jax.random.randint(key_order, (PROW, PCOL, PROW, SL), 0, 1 << 16) * SL + jnp.arange(SL, dtype=jnp.int32)
    first = (jnp.arange(PROW, dtype=jnp.int32)[:, None, None, None] == 0) & (jnp.arange(PCOL, dtype=jnp.int32)[None, :, None, None] == 0)
    last_source = jnp.arange(PROW, dtype=jnp.int32)[None, None, :, None] == PROW - 1
    last_slot = jnp.arange(SL, dtype=jnp.int32)[None, None, None, :] == SL - 1
    scores = jnp.where(first & last_source & last_slot, -1, scores)
    order = jnp.argsort(scores, axis=-1, stable=True).astype(jnp.int32)
    allowed = order[..., :CAP]
    source = jax.random.randint(key_source, shape, 0, PROW)
    pick = jax.random.randint(key_pick, shape, 0, CAP)
    term = jnp.arange(TERMS, dtype=jnp.int32)[None, None, None, :]
    head = (jnp.arange(PROW, dtype=jnp.int32)[:, None, None, None] == 0) & (jnp.arange(PCOL, dtype=jnp.int32)[None, :, None, None] == 0) & (jnp.arange(SL, dtype=jnp.int32)[None, None, :, None] == 0)
    source = jnp.where(head & (term < CAP), 0, source)
    pick = jnp.where(head & (term < CAP), term, pick)
    source = jnp.where(head & (term == CAP), PROW - 1, source)
    pick = jnp.where(head & (term == CAP), 0, pick)
    table = allowed.reshape(PROW, PCOL, 1, PROW * CAP)
    table = jnp.broadcast_to(table, (PROW, PCOL, SL, PROW * CAP))
    slot = jnp.take_along_axis(table, (source * CAP + pick).astype(jnp.int32), axis=-1)
    right_index = source * SL + slot
    return jnp.stack([left_index, right_index], axis=-1).astype(jnp.int32)


def draw_term_count(key, part):
    key = jax.random.fold_in(key, 23)
    key_level, key_spread, key_spot = jax.random.split(key, 3)
    level = jax.random.randint(key_level, (PROW, PCOL, 1), TERMS // 2, TERMS + 1)
    spread = jax.random.randint(key_spread, (PROW, PCOL, SL), 0, 1 << 20)
    counts = 1 + spread % level
    total = PROW * PCOL * SL
    spot = jax.random.randint(key_spot, (), 0, total - 1)
    position = jnp.arange(total, dtype=jnp.int32).reshape(PROW, PCOL, SL)
    counts = jnp.where(position == spot, TERMS, counts)
    counts = jnp.where(position == total - 1, 1, counts)
    return counts.astype(jnp.int32)


def levels(key, extent, shards, low, high):
    gain = 1.0
    for dim, shards_of in shards:
        heights = jax.random.uniform(jax.random.fold_in(jax.random.fold_in(key, 6), dim), (shards_of,), jnp.float32, low / len(shards), high / len(shards))
        gain = gain * jnp.repeat(jnp.exp(heights), extent[dim] // shards_of).reshape((-1,) + (1,) * (len(extent) - 1 - dim))
    return gain


def centred(rng, dims, scale, most, cuts=(), kind=jnp.bfloat16):
    drawn = scale * jax.random.normal(rng, dims, jnp.float32)
    if cuts:
        drawn = drawn * levels(rng, dims, cuts, -0.22, 0.18)
    return jnp.clip(drawn, -most, most).astype(kind)


def setup_inputs(seed: int = 0, part: int = 0) -> dict:
    streams_of = jax.random.split(jax.random.key(seed), 4)
    part_splits = jax.random.split(jax.random.fold_in(streams_of[3], part), 4)
    blocks = centred(part_splits[0], (PROW, PCOL, SL, B, B), 0.15, 0.8984375, ((0, 4), (1, 4)))
    pairs = draw_pairs(jax.random.fold_in(jax.random.fold_in(streams_of[3], part), 71), part)
    term_count = draw_term_count(jax.random.fold_in(jax.random.fold_in(streams_of[3], part), 71), part)
    return dict(blocks=blocks, pairs=pairs, term_count=term_count)


def panel_product(left_blocks, right_blocks, pairs, term_count):
    def one_device(index):
        row_index = index // PCOL
        col_index = index % PCOL
        left_panel = left_blocks[row_index].reshape(PCOL * SL, B, B)
        right_panel = right_blocks[:, col_index].reshape(PROW * SL, B, B)
        pairing = pairs[row_index, col_index]
        active = (jnp.arange(TERMS, dtype=jnp.int32)[None, :] < term_count[row_index, col_index][:, None]).astype(jnp.float32)
        left_stack = left_panel[pairing[:, :, 0]].astype(jnp.float32) * active[:, :, None, None]
        right_stack = right_panel[pairing[:, :, 1]].astype(jnp.float32)
        return jnp.einsum("stij,stjk->sik", left_stack, right_stack)

    result = lax.map(one_device, jnp.arange(PROW * PCOL, dtype=jnp.int32))
    return result.reshape(PROW, PCOL, SL, B, B)


def reference(blocks, pairs, term_count):
    square = panel_product(blocks, blocks, pairs, term_count)
    square_stored = square.astype(jnp.bfloat16)
    cubed = panel_product(square_stored, blocks, pairs, term_count)
    return (3.0 * square - 2.0 * cubed).astype(jnp.bfloat16)
```

```python
import functools

import jax
import jax.numpy as jnp
from jax import lax
from jax.experimental import pallas as pl
from jax.experimental.pallas import tpu as pltpu
from jax.sharding import PartitionSpec as P

CAP = 8
LANES = 128
SMEM = pl.BlockSpec(memory_space=pltpu.SMEM)
VMEM = pl.BlockSpec(memory_space=pltpu.VMEM)


def params():
    return pltpu.CompilerParams(vmem_limit_bytes=48 * 1024 * 1024)


def cube_like(extent):
    return extent & (extent - 1) == 0


def prepare_kernel(slots, rows, cols, relative, pairs_ref, count_ref, table_ref, *request_refs):
    terms = pairs_ref.shape[2]
    row, col = lax.axis_index("row"), lax.axis_index("col")
    keys = rows * slots
    key = lax.broadcasted_iota(jnp.int32, (keys, terms), 0)
    source, slot = key // slots, key % slots
    if relative:
        wanted = ((row - source + rows) % rows) * slots + slot
    else:
        wanted = key
    used = jnp.zeros((keys, terms), jnp.int32)
    for s in range(slots):
        used = jnp.where(pairs_ref[s, 1:2, :] == wanted, 1, used)
    used = jnp.max(used, axis=1, keepdims=True)
    across = lax.broadcasted_iota(jnp.int32, (keys, keys), 1)
    down = lax.broadcasted_iota(jnp.int32, (keys, keys), 0)
    before = (across // slots == down // slots) & (across < down)
    rank = jnp.dot(
        before.astype(jnp.bfloat16),
        jnp.broadcast_to(used, (keys, LANES)).astype(jnp.bfloat16),
        preferred_element_type=jnp.float32,
    ).astype(jnp.int32)
    used = jnp.broadcast_to(used, (keys, LANES))
    lane = lax.broadcasted_iota(jnp.int32, (keys, LANES), 1)
    slot = lax.broadcasted_iota(jnp.int32, (keys, LANES), 0) % slots
    listed = jnp.where((used > 0) & (rank == lane), slot, 0)
    if relative:
        for distance, request_ref in enumerate(request_refs, 1):
            part = listed[distance * slots : (distance + 1) * slots]
            request_ref[...] = jnp.sum(part, axis=0, keepdims=True)
    else:
        request_refs[0][...] = jnp.sum(listed.reshape(rows, slots, LANES), axis=1)
    source, slot = key // slots, key % slots
    if relative:
        place = jnp.where(source == 0, slot, slots + (source - 1) * CAP + rank[:, :terms])
    else:
        place = jnp.where(source == row, slot, slots + source * CAP + rank[:, :terms])
    counts = count_ref[...]
    term = lax.broadcasted_iota(jnp.int32, (1, terms), 1)
    for s in range(slots):
        left = pairs_ref[s, 0:1, :]
        if cube_like(cols):
            left = ((left // slots) ^ col) * slots + left % slots
        active = term < counts[:, s : s + 1]
        table_ref[s : s + 1, :] = jnp.where(active, left, cols * slots)
        hit = pairs_ref[s, 1:2, :] == wanted
        table_ref[slots + s : slots + s + 1, :] = jnp.sum(
            jnp.where(hit, place, 0), axis=0, keepdims=True
        )


def pick_kernel(sets, *refs):
    asked_refs, blocks_ref, out_refs = refs[:sets], refs[sets], refs[sets + 1 :]
    for asked_ref, out_ref in zip(asked_refs, out_refs):
        for group in range(asked_ref.shape[0]):
            for place in range(CAP):
                out_ref[group * CAP + place] = blocks_ref[asked_ref[group, place]]


def fill(panel_ref, piece_refs):
    at = 0
    for piece_ref in piece_refs:
        count = piece_ref.shape[0]
        panel_ref[at : at + count] = piece_ref[...]
        at += count
    return at


def sum_products(table_ref, left_ref, right_ref, slots, terms, finish):
    def body(step, carry):
        for s in (2 * step, 2 * step + 1):
            left = jnp.concatenate([left_ref[table_ref[s, t]] for t in range(terms)], axis=1)
            right = jnp.concatenate(
                [right_ref[table_ref[slots + s, t]] for t in range(terms)], axis=0
            )
            finish(s, jnp.dot(left, right, preferred_element_type=jnp.float32))
        return carry

    lax.fori_loop(0, slots // 2, body, 0)


def square_kernel(lefts, table_ref, *refs):
    left_refs, right_refs = refs[:lefts], refs[lefts:-4]
    square_ref, stored_ref, left_ref, right_ref = refs[-4:]
    slots, terms = square_ref.shape[0], table_ref.shape[1]
    at = fill(left_ref, left_refs)
    left_ref[at] = jnp.zeros(left_ref.shape[1:], left_ref.dtype)
    fill(right_ref, right_refs)

    def finish(s, value):
        square_ref[s] = value
        stored_ref[s] = value.astype(jnp.bfloat16)

    sum_products(table_ref, left_ref, right_ref, slots, terms, finish)


def cube_kernel(lefts, table_ref, square_ref, *refs):
    left_refs, right_refs = refs[:lefts], refs[lefts:-3]
    out_ref, left_ref, right_ref = refs[-3:]
    slots, terms = square_ref.shape[0], table_ref.shape[1]
    at = fill(left_ref, left_refs)
    left_ref[at] = jnp.zeros(left_ref.shape[1:], left_ref.dtype)
    fill(right_ref, right_refs)

    def finish(s, value):
        out_ref[s] = (3.0 * square_ref[s] - 2.0 * value).astype(jnp.bfloat16)

    sum_products(table_ref, left_ref, right_ref, slots, terms, finish)


def row_panel(blocks, cols):
    if not cube_like(cols):
        return [lax.all_gather(blocks, "col", axis=0, tiled=True)]
    pieces = {0: blocks}
    bit = cols // 2
    while bit:
        for k in list(pieces):
            pieces[k ^ bit] = lax.ppermute(pieces[k], "col", [(i, i ^ bit) for i in range(cols)])
        bit //= 2
    return [pieces[k] for k in range(cols)]


def per_device(blocks, pairs, term_count):
    extent = blocks.shape[-1]
    slots, terms = pairs.shape[2], pairs.shape[3]
    rows, cols = lax.axis_size("row"), lax.axis_size("col")
    relative = rows <= 4
    local = blocks.reshape(slots, extent, extent)
    pairing = jnp.swapaxes(pairs.reshape(slots, terms, 2), 1, 2)
    request_shapes = [(1, LANES)] * (rows - 1) if relative else [(rows, LANES)]
    table, *requests = pl.pallas_call(
        functools.partial(prepare_kernel, slots, rows, cols, relative),
        out_shape=[jax.ShapeDtypeStruct((2 * slots, terms), jnp.int32)]
        + [jax.ShapeDtypeStruct(shape, jnp.int32) for shape in request_shapes],
        in_specs=[VMEM, VMEM],
        out_specs=[VMEM] * (1 + len(request_shapes)),
        compiler_params=params(),
    )(pairing, term_count.reshape(1, slots))
    if relative:
        asked = [
            lax.ppermute(request, "row", [(i, (i - d) % rows) for i in range(rows)])
            for d, request in enumerate(requests, 1)
        ]
    else:
        asked = [lax.all_to_all(requests[0], "row", split_axis=0, concat_axis=0, tiled=True)]
    picked = pl.pallas_call(
        functools.partial(pick_kernel, len(asked)),
        out_shape=[
            jax.ShapeDtypeStruct((a.shape[0] * CAP, extent, extent), blocks.dtype) for a in asked
        ],
        in_specs=[SMEM] * len(asked) + [VMEM],
        out_specs=[VMEM] * len(asked),
        compiler_params=params(),
    )(*asked, local)
    if relative:
        far = [
            lax.ppermute(piece, "row", [(i, (i + d) % rows) for i in range(rows)])
            for d, piece in enumerate(picked, 1)
        ]
    else:
        far = [lax.all_to_all(picked[0], "row", split_axis=0, concat_axis=0, tiled=True)]
    rights = [local, *far]
    right_count = sum(piece.shape[0] for piece in rights)
    scratch = [
        pltpu.VMEM((cols * slots + 1, extent, extent), blocks.dtype),
        pltpu.VMEM((right_count, extent, extent), blocks.dtype),
    ]
    whole = (slots, extent, extent)
    lefts = row_panel(local, cols)
    square, stored = pl.pallas_call(
        functools.partial(square_kernel, len(lefts)),
        out_shape=[
            jax.ShapeDtypeStruct(whole, jnp.float32),
            jax.ShapeDtypeStruct(whole, jnp.bfloat16),
        ],
        in_specs=[SMEM] + [VMEM] * (len(lefts) + len(rights)),
        out_specs=[VMEM, VMEM],
        scratch_shapes=scratch,
        compiler_params=params(),
    )(table, *lefts, *rights)
    lefts = row_panel(stored, cols)
    purified = pl.pallas_call(
        functools.partial(cube_kernel, len(lefts)),
        out_shape=jax.ShapeDtypeStruct(whole, jnp.bfloat16),
        in_specs=[SMEM] + [VMEM] * (1 + len(lefts) + len(rights)),
        out_specs=VMEM,
        scratch_shapes=scratch,
        compiler_params=params(),
    )(table, square, *lefts, *rights)
    return purified.reshape(blocks.shape)


def solution(mesh):
    placed = (
        P(("sys", "row"), "col", None, None, None),
        P(("sys", "row"), "col", None, None, None),
        P(("sys", "row"), "col", None),
    )
    return jax.shard_map(
        per_device,
        mesh=mesh,
        in_specs=placed,
        out_specs=P(("sys", "row"), "col", None, None, None),
        check_vma=False,
    )
```

```python
import functools
import math

import jax
import jax.numpy as jnp
from jax import lax
from jax.experimental import pallas as pl
from jax.experimental.pallas import tpu as pltpu
from jax.sharding import PartitionSpec as P

CAP = 8
LANES = 128
MIB = 1 << 20
CHUNK = 16
FIELD = 1024
SMEM = pl.BlockSpec(memory_space=pltpu.SMEM)
VMEM = pl.BlockSpec(memory_space=pltpu.VMEM)


def params(limit):
    return pltpu.CompilerParams(vmem_limit_bytes=limit)


def cost(us):
    return pl.CostEstimate(
        flops=int(us * 10**9) + 10**5, bytes_accessed=int(us * 3 * 10**6) + 10**3, transcendentals=0
    )


def is_power(extent):
    return extent & (extent - 1) == 0


def prepare_kernel(slots, rows, cols, line, pairs_ref, table_ref, request_ref):
    terms = pairs_ref.shape[2]
    row, col = lax.axis_index("row"), lax.axis_index("col")
    keys = rows * slots
    key = lax.broadcasted_iota(jnp.int32, (keys, terms), 0)
    used = jnp.zeros((keys, terms), jnp.int32)
    for s in range(slots):
        used = jnp.where(pairs_ref[s, 1:2, :] == key, 1, used)
    used = jnp.max(used, axis=1, keepdims=True)
    across = lax.broadcasted_iota(jnp.int32, (keys, keys), 1)
    down = lax.broadcasted_iota(jnp.int32, (keys, keys), 0)
    before = (across // slots == down // slots) & (across < down)
    used = jnp.broadcast_to(used, (keys, LANES))
    rank = jnp.dot(
        before.astype(jnp.bfloat16),
        used.astype(jnp.bfloat16),
        preferred_element_type=jnp.float32,
    ).astype(jnp.int32)
    lane = lax.broadcasted_iota(jnp.int32, (keys, LANES), 1)
    place = lax.broadcasted_iota(jnp.int32, (keys, LANES), 0)
    listed = jnp.where((used > 0) & (rank == lane), place % slots, 0)
    source, slot, rank = key // slots, key % slots, rank[:, :terms]
    if line:
        far = jnp.abs(place // slots - row)
        for distance in (2, 3):
            part = jnp.where(far == distance, listed, 0)
            request_ref[distance - 2 : distance - 1, :] = jnp.sum(part, axis=0, keepdims=True)
        away = jnp.abs(source - row)
        is_end = (row == 0) | (row == rows - 1)
        place = jnp.where(away == 0, slot, 2 * slots + slot)
        place = jnp.where(source == row ^ 1, slots + slot, place)
        place = jnp.where(away == 2, 3 * slots + jnp.where(is_end, rank, slot), place)
        place = jnp.where(away == 3, 3 * slots + CAP + rank, place)
    else:
        request_ref[...] = jnp.sum(listed.reshape(rows, slots, LANES), axis=1)
        place = jnp.where(source == row, slot, slots + source * CAP + rank)
    for s in range(slots):
        left = pairs_ref[s, 0:1, :]
        if is_power(cols):
            left = ((left // slots) ^ col) * slots + left % slots
        hit = pairs_ref[s, 1:2, :] == key
        right = jnp.sum(jnp.where(hit, place, 0), axis=0, keepdims=True)
        table_ref[s : s + 1, :] = left + FIELD * (right + FIELD * s)


def plan_kernel(near, close, blank, table_ref, count_ref, plan_ref, total_ref):
    slots = table_ref.shape[0]
    room = plan_ref.shape[0] // 4

    def blank_of(s):
        return blank + FIELD * FIELD * s

    def block(s, ends):
        def term(t, ends):
            word = table_ref[s, t]
            is_near = ((word // FIELD) % FIELD < near).astype(jnp.int32)
            is_close = (word % FIELD < close).astype(jnp.int32)
            for end in ends:
                plan_ref[end] = word
            a, b, c, d = ends
            return a + is_near, b + 1 - is_near, c + is_close, d + 1 - is_close

        ends = lax.fori_loop(0, count_ref[0, s], term, ends)
        for end in ends:
            plan_ref[end] = blank_of(s)
        return tuple(end + end % 2 for end in ends)

    ends = lax.fori_loop(0, slots, block, tuple(jnp.int32(i * room) for i in range(4)))
    for i, end in enumerate(ends):
        total_ref[i] = end - i * room

        def pad(j, carry, end=end):
            plan_ref[end + j] = blank
            return carry

        lax.fori_loop(0, 2 * CHUNK, pad, 0)


def halves(first, second):
    half = first.shape[-1] // 2
    return (
        jnp.concatenate([first[:, :half], second[:, :half]], axis=1),
        jnp.concatenate([first[:, half:], second[:, half:]], axis=1),
    )


def pick(asked_ref, group, source_ref, left_ref, right_ref):
    for p in range(CAP // 2):
        first = source_ref[asked_ref[group, 2 * p]]
        second = source_ref[asked_ref[group, 2 * p + 1]]
        at = group * (CAP // 2) + p
        left_ref[at], right_ref[at] = halves(first, second)


def pick_far_kernel(asked_ref, blocks_ref, left_ref, right_ref):
    for group in range(asked_ref.shape[0]):
        pick(asked_ref, group, blocks_ref, left_ref, right_ref)


def relay_kernel(after_ref, partner_ref, low_ref, high_ref):
    row = lax.axis_index("row")

    @pl.when((row == 1) | (row == 2))
    def _():
        for p in range(low_ref.shape[0]):
            low_ref[p], high_ref[p] = halves(partner_ref[2 * p], partner_ref[2 * p + 1])


def early_kernel(asked_ref, middle_ref, out_ref):
    row = lax.axis_index("row")

    @pl.when((row == 1) | (row == 2))
    def _():
        pick(asked_ref, 0, middle_ref, out_ref, out_ref.at[CAP // 2 :])


def late_kernel(asked_ref, passed_ref, after_ref, out_ref):
    row = lax.axis_index("row")
    half = passed_ref.shape[-1] // 2

    def side(place):
        slot = asked_ref[1, place]
        both = passed_ref[slot // 2]
        return jnp.where(slot % 2 == 0, both, turned(both))[:, :half]

    @pl.when((row == 1) | (row == 2))
    def _():
        for p in range(CAP // 2):
            out_ref[p] = jnp.concatenate([side(2 * p), side(2 * p + 1)], axis=1)


def fill(panel_ref, piece_refs):
    at = 0
    for piece_ref in piece_refs:
        count = piece_ref.shape[0]
        panel_ref[at : at + count] = piece_ref[...]
        at += count
    return at


def turned(block):
    half = block.shape[-1] // 2
    return jnp.concatenate([block[:, half:], block[:, :half]], axis=1)


def add_products(plan_ref, total_ref, which, left_ref, right_ref, sum_ref, left_shift=0):
    room = plan_ref.shape[0] // 4

    def step(c, carry):
        for p in range(CHUNK):
            first = plan_ref[which * room + 2 * (c * CHUNK + p)]
            second = plan_ref[which * room + 2 * (c * CHUNK + p) + 1]
            left = jnp.concatenate(
                [left_ref[word % FIELD - left_shift] for word in (first, second)], axis=1
            )
            right = jnp.concatenate(
                [right_ref[(word // FIELD) % FIELD] for word in (first, second)], axis=0
            )
            sum_ref[first // (FIELD * FIELD)] += jnp.dot(
                left, right, preferred_element_type=jnp.float32
            )
        return carry

    lax.fori_loop(0, (total_ref[which] + 2 * CHUNK - 1) // (2 * CHUNK), step, 0)


def near_kernel(lefts, plan_ref, total_ref, *refs):
    left_refs, right_refs = refs[:lefts], refs[lefts:-4]
    sum_ref, left_ref, token_ref, right_ref = refs[-4:]
    token_ref[...] = jnp.zeros(token_ref.shape, token_ref.dtype)
    at = fill(left_ref, left_refs)
    left_ref[at] = jnp.zeros(left_ref.shape[1:], left_ref.dtype)
    fill(right_ref, right_refs)
    sum_ref[...] = jnp.zeros(sum_ref.shape, sum_ref.dtype)
    add_products(plan_ref, total_ref, 0, left_ref, right_ref, sum_ref)


def unpack(panel_ref, at, piece_ref, first, count):
    for p in range(count):
        both = piece_ref[first + p]
        panel_ref[at + 2 * p] = both
        panel_ref[at + 2 * p + 1] = turned(both)


def far_kernel(start, turn, line, plan_ref, total_ref, near_ref, left_ref, after_ref, *refs):
    far_refs = refs[:-3]
    sum_ref, stored_ref, right_ref = refs[-3:]
    right_ref[0] = jnp.zeros(right_ref.shape[1:], right_ref.dtype)
    if line:
        row = lax.axis_index("row")

        @pl.when((row == 1) | (row == 2))
        def _():
            unpack(right_ref, start, far_refs[0], 0, far_refs[0].shape[0])

        @pl.when((row == 0) | (row == 3))
        def _():
            unpack(right_ref, start, far_refs[1], turn * CAP // 2, CAP // 2)
            unpack(right_ref, start + CAP, far_refs[2], 0, CAP // 2)
    else:
        unpack(right_ref, start, far_refs[0], 0, far_refs[0].shape[0])
    for s in range(sum_ref.shape[0]):
        sum_ref[s] = turned(near_ref[s]) if turn else near_ref[s]
    add_products(plan_ref, total_ref, 1, left_ref, right_ref, sum_ref)
    half = sum_ref.shape[-1] // 2
    for p in range(stored_ref.shape[0]):
        both = [sum_ref[2 * p][:, :half], sum_ref[2 * p + 1][:, :half]]
        stored_ref[p] = jnp.concatenate(both, axis=1).astype(jnp.bfloat16)


def join(panel_ref, at, low_ref, high_ref, first, second, count):
    for p in range(count):
        panel_ref[at + 2 * p], panel_ref[at + 2 * p + 1] = halves(
            low_ref[first + p], high_ref[second + p]
        )


def close_kernel(closes, nears, line, blank, plan_ref, total_ref, after_ref, *refs):
    refs, (sum_ref, right_ref, token_ref, left_ref) = refs[:-4], refs[-4:]
    sums, refs = refs[:2], refs[2:]
    lows, highs, refs = refs[:closes], refs[closes : 2 * closes], refs[2 * closes :]
    near_refs, refs = refs[:nears], refs[nears:]
    token_ref[...] = jnp.zeros(token_ref.shape, token_ref.dtype)
    at = 0
    for low_ref, high_ref in zip(lows, highs):
        join(left_ref, at, low_ref, high_ref, 0, 0, low_ref.shape[0])
        at += 2 * low_ref.shape[0]
    left_ref[blank] = jnp.zeros(left_ref.shape[1:], left_ref.dtype)
    at = fill(right_ref, near_refs)
    if line:
        passed_low_ref, passed_high_ref, early_ref, late_low_ref, late_high_ref = refs
        row = lax.axis_index("row")

        @pl.when((row == 1) | (row == 2))
        def _():
            join(right_ref, at, passed_low_ref, passed_high_ref, 0, 0, passed_low_ref.shape[0])

        @pl.when((row == 0) | (row == 3))
        def _():
            join(right_ref, at, early_ref, early_ref, 0, CAP // 2, CAP // 2)
            join(right_ref, at + CAP, late_low_ref, late_high_ref, 0, 0, CAP // 2)
    else:
        join(right_ref, at, refs[0], refs[1], 0, 0, refs[0].shape[0])
    half = sum_ref.shape[-1] // 2
    for s in range(sum_ref.shape[0]):
        both = [sums[0][s][:, :half], sums[1][s][:, :half]]
        sum_ref[s] = -1.5 * jnp.concatenate(both, axis=1)
    add_products(plan_ref, total_ref, 2, left_ref, right_ref, sum_ref)


def distant_kernel(distants, close, plan_ref, total_ref, close_ref, right_ref, *refs):
    lows, highs = refs[:distants], refs[distants : 2 * distants]
    out_ref, left_ref, sum_ref = refs[-3:]
    at = 0
    for low_ref, high_ref in zip(lows, highs):
        join(left_ref, at, low_ref, high_ref, 0, 0, low_ref.shape[0])
        at += 2 * low_ref.shape[0]
    left_ref[at] = jnp.zeros(left_ref.shape[1:], left_ref.dtype)
    sum_ref[...] = close_ref[...]
    add_products(plan_ref, total_ref, 3, left_ref, right_ref, sum_ref, close)
    out_ref[...] = (-2.0 * sum_ref[...]).astype(jnp.bfloat16)


def nothing_kernel(value_ref, after_ref, out_ref):
    pass


def after(value, earlier, us=0):
    return pl.pallas_call(
        nothing_kernel,
        out_shape=jax.ShapeDtypeStruct(value.shape, value.dtype),
        in_specs=[VMEM, VMEM],
        out_specs=VMEM,
        input_output_aliases={0: 0},
        compiler_params=params(8 * MIB),
        cost_estimate=cost(us),
    )(value, earlier)


def row_panel(blocks, cols, earlier=None):
    if not is_power(cols):
        return [lax.all_gather(blocks, "col", axis=0, tiled=True)]
    pieces = spread(blocks, cols // 2, cols)
    if cols > 1:
        piece = cross(blocks, cols)
        if earlier is not None:
            piece = after(piece, earlier)
        pieces += spread(piece, cols // 2, cols)
    return pieces


def cross(blocks, cols):
    return lax.ppermute(blocks, "col", [(i, i ^ (cols // 2)) for i in range(cols)])


def per_device(blocks, pairs, term_count):
    extent = blocks.shape[-1]
    slots, terms = pairs.shape[2], pairs.shape[3]
    rows, cols = lax.axis_size("row"), lax.axis_size("col")
    line = rows == 4
    local = blocks.reshape(slots, extent, extent)
    pairing = jnp.swapaxes(pairs.reshape(slots, terms, 2), 1, 2)

    def call(kernel, outs, ins, scratch=(), smem=0, out_smem=False, us=2):
        sizes = [(a.shape, a.dtype) for a in ins[smem:]] + [(a.shape, a.dtype) for a in scratch]
        sizes += [] if out_smem else outs
        vmem = 4 * MIB + sum(math.prod(shape) * jnp.dtype(dtype).itemsize for shape, dtype in sizes)
        return pl.pallas_call(
            kernel,
            out_shape=[jax.ShapeDtypeStruct(shape, dtype) for shape, dtype in outs],
            in_specs=[SMEM] * smem + [VMEM] * (len(ins) - smem),
            out_specs=[SMEM if out_smem else VMEM] * len(outs),
            scratch_shapes=list(scratch),
            compiler_params=params(vmem),
            cost_estimate=cost(us),
        )(*ins)

    def blocks_of(count):
        return ((count, extent, extent), local.dtype)

    whole = ((slots, extent, extent), jnp.float32)
    requests = ((2 if line else rows, LANES), jnp.int32)
    table, request = call(
        functools.partial(prepare_kernel, slots, rows, cols, line),
        [((slots, terms), jnp.int32), requests],
        [pairing],
    )
    paired = is_power(cols) and cols > 1
    close = cols // 2 * slots if paired else cols * slots
    blank = cols * slots
    near_count = 3 * slots if line else slots
    far_count = 2 * CAP if line else rows * CAP
    right_count = near_count + far_count
    room = slots * terms + 4 * CHUNK
    plan, total = call(
        functools.partial(plan_kernel, near_count, close, blank),
        [((4 * room,), jnp.int32), ((4,), jnp.int32)],
        [table, term_count.reshape(1, slots)],
        smem=2,
        out_smem=True,
    )
    if line:
        outer = [(i, i ^ 1) for i in range(rows)]
        inner = [(1, 2), (2, 1)]
        partner = lax.ppermute(local, "row", outer)
        middle = lax.ppermute(local, "row", inner)
        asked = lax.ppermute(request, "row", outer)
        halved = call(relay_kernel, [blocks_of(slots // 2)] * 2, [total, partner], smem=1)
        passed = [lax.ppermute(piece, "row", inner) for piece in halved]
        (early,) = call(early_kernel, [blocks_of(CAP)], [asked, middle], smem=1)
        early = lax.ppermute(early, "row", outer)
        nears = [local, partner, middle]
        token = halved[0]
    else:
        asked = lax.all_to_all(request, "row", split_axis=0, concat_axis=0, tiled=True)
        picked = call(pick_far_kernel, [blocks_of(rows * CAP // 2)] * 2, [asked, local], smem=1)
        token = picked[0]
        nears = [local]
        fars = [
            [lax.all_to_all(piece, "row", split_axis=0, concat_axis=0, tiled=True)]
            for piece in picked
        ]
        far_panel = [fars[0][0], fars[1][0]]
    lefts = row_panel(local, cols, token)

    def panel(count):
        return pltpu.VMEM((count, extent, extent), local.dtype)

    near, left_panel, token = call(
        functools.partial(near_kernel, len(lefts)),
        [whole, blocks_of(blank + 1), ((8, LANES), jnp.float32)],
        [plan, total, *lefts, *nears],
        [panel(near_count)],
        smem=2,
    )
    sums, squares, crossed, lates = [], [], [], []
    for turn in range(2):
        if line:
            (late,) = call(late_kernel, [blocks_of(CAP // 2)], [asked, passed[turn], token], smem=1)
            token = late
            lates.append(lax.ppermute(late, "row", outer))
            far = [passed[turn], early, lates[turn]]
        else:
            far = fars[turn]
        total_half, stored = call(
            functools.partial(far_kernel, near_count, turn, line),
            [whole, blocks_of(slots // 2)],
            [plan, total, near, left_panel, (squares or [near])[-1], *far],
            [panel(right_count)],
            smem=2,
        )
        sums.append(total_half)
        squares.append(stored)
        if paired:
            crossed.append(cross(stored, cols))
    if line:
        far_panel = [*passed, early, *lates]
    if paired:
        closes = [spread(stored, cols // 2, cols) for stored in squares]
    else:
        closes = [row_panel(stored, cols) for stored in squares]
        crossed = squares
    if paired:
        crossed[0] = after(crossed[0], token, 0.3)
    partial_sum, right_panel, token = call(
        functools.partial(close_kernel, len(closes[0]), len(nears), line, blank),
        [whole, blocks_of(right_count), ((8, LANES), jnp.float32)],
        [plan, total, crossed[0], *sums, *closes[0], *closes[1], *nears, *far_panel],
        [panel(blank + 1)],
        smem=2,
        us=0,
    )
    distants = [[], []]
    if paired:
        crossed[1] = after(crossed[1], token)
        distants = [spread(piece, cols // 2, cols) for piece in crossed]
    (purified,) = call(
        functools.partial(distant_kernel, len(distants[0]), close),
        [((slots, extent, extent), local.dtype)],
        [plan, total, partial_sum, right_panel, *distants[0], *distants[1]],
        [panel(blank + 1 - close), pltpu.VMEM(*whole)],
        smem=2,
    )
    return purified.reshape(blocks.shape)


def spread(blocks, extent, cols):
    pieces = {0: blocks}
    bit = extent // 2
    while bit:
        for k in list(pieces):
            pieces[k ^ bit] = lax.ppermute(pieces[k], "col", [(i, i ^ bit) for i in range(cols)])
        bit //= 2
    return [pieces[k] for k in sorted(pieces)]


def solution(mesh):
    placed = (
        P(("sys", "row"), "col", None, None, None),
        P(("sys", "row"), "col", None, None, None),
        P(("sys", "row"), "col", None),
    )
    return jax.shard_map(
        per_device,
        mesh=mesh,
        in_specs=placed,
        out_specs=P(("sys", "row"), "col", None, None, None),
        check_vma=False,
    )
```

```python
import functools
import math

import jax
import jax.numpy as jnp
from jax import lax
from jax.experimental import pallas as pl
from jax.experimental.pallas import tpu as pltpu
from jax.sharding import PartitionSpec as P

CAP = 8
LANES = 128
MIB = 1 << 20
CHUNK = 16
FIELD = 1024
SMEM = pl.BlockSpec(memory_space=pltpu.SMEM)
VMEM = pl.BlockSpec(memory_space=pltpu.VMEM)
ANY = pl.BlockSpec(memory_space=pl.ANY)


def params(limit):
    return pltpu.CompilerParams(vmem_limit_bytes=limit)


def cost(us):
    return pl.CostEstimate(
        flops=int(us * 10**9) + 10**5, bytes_accessed=int(us * 3 * 10**6) + 10**3, transcendentals=0
    )


def is_power(extent):
    return extent & (extent - 1) == 0


def prepare_kernel(slots, rows, cols, line, pairs_ref, table_ref, request_ref):
    terms = pairs_ref.shape[2]
    row, col = lax.axis_index("row"), lax.axis_index("col")
    keys = rows * slots
    key = lax.broadcasted_iota(jnp.int32, (keys, terms), 0)
    used = jnp.zeros((keys, terms), jnp.int32)
    for s in range(slots):
        used = jnp.where(pairs_ref[s, 1:2, :] == key, 1, used)
    used = jnp.max(used, axis=1, keepdims=True)
    across = lax.broadcasted_iota(jnp.int32, (keys, keys), 1)
    down = lax.broadcasted_iota(jnp.int32, (keys, keys), 0)
    before = (across // slots == down // slots) & (across < down)
    used = jnp.broadcast_to(used, (keys, LANES))
    rank = jnp.dot(
        before.astype(jnp.bfloat16),
        used.astype(jnp.bfloat16),
        preferred_element_type=jnp.float32,
    ).astype(jnp.int32)
    lane = lax.broadcasted_iota(jnp.int32, (keys, LANES), 1)
    place = lax.broadcasted_iota(jnp.int32, (keys, LANES), 0)
    listed = jnp.where((used > 0) & (rank == lane), place % slots, 0)
    source, slot, rank = key // slots, key % slots, rank[:, :terms]
    if line:
        far = jnp.abs(place // slots - row)
        for distance in (2, 3):
            part = jnp.where(far == distance, listed, 0)
            request_ref[distance - 2 : distance - 1, :] = jnp.sum(part, axis=0, keepdims=True)
        away = jnp.abs(source - row)
        is_end = (row == 0) | (row == rows - 1)
        place = jnp.where(away == 0, slot, 2 * slots + slot)
        place = jnp.where(source == row ^ 1, slots + slot, place)
        place = jnp.where(away == 2, 3 * slots + jnp.where(is_end, rank, slot), place)
        place = jnp.where(away == 3, 3 * slots + CAP + rank, place)
    else:
        request_ref[...] = jnp.sum(listed.reshape(rows, slots, LANES), axis=1)
        place = jnp.where(source == row, slot, slots + source * CAP + rank)
    for s in range(slots):
        left = pairs_ref[s, 0:1, :]
        if is_power(cols):
            left = ((left // slots) ^ col) * slots + left % slots
        hit = pairs_ref[s, 1:2, :] == key
        right = jnp.sum(jnp.where(hit, place, 0), axis=0, keepdims=True)
        table_ref[s : s + 1, :] = left + FIELD * (right + FIELD * s)


def plan_kernel(near, close, blank, table_ref, count_ref, plan_ref, token_ref):
    slots = table_ref.shape[0]
    room = plan_ref.shape[0] // 4 - LANES // 4
    token_ref[0] = 0

    def blank_of(s):
        return blank + FIELD * FIELD * s

    def block(s, ends):
        def term(t, ends):
            word = table_ref[s, t]
            is_near = ((word // FIELD) % FIELD < near).astype(jnp.int32)
            is_close = (word % FIELD < close).astype(jnp.int32)
            for end in ends:
                plan_ref[end] = word
            a, b, c, d = ends
            return a + is_near, b + 1 - is_near, c + is_close, d + 1 - is_close

        ends = lax.fori_loop(0, count_ref[0, s], term, ends)
        for end in ends:
            plan_ref[end] = blank_of(s)
        return tuple(end + end % 2 for end in ends)

    ends = lax.fori_loop(0, slots, block, tuple(jnp.int32(i * room) for i in range(4)))
    for i, end in enumerate(ends):
        plan_ref[4 * room + i] = end - i * room

        def pad(j, carry, end=end):
            plan_ref[end + j] = blank
            return carry

        lax.fori_loop(0, 2 * CHUNK, pad, 0)


def halves(first, second):
    half = first.shape[-1] // 2
    return (
        jnp.concatenate([first[:, :half], second[:, :half]], axis=1),
        jnp.concatenate([first[:, half:], second[:, half:]], axis=1),
    )


def pick(asked_ref, group, source_ref, left_ref, right_ref):
    for p in range(CAP // 2):
        first = source_ref[asked_ref[group, 2 * p]]
        second = source_ref[asked_ref[group, 2 * p + 1]]
        at = group * (CAP // 2) + p
        left_ref[at], right_ref[at] = halves(first, second)


def pick_far_kernel(asked_ref, blocks_ref, left_ref, right_ref):
    for group in range(asked_ref.shape[0]):
        pick(asked_ref, group, blocks_ref, left_ref, right_ref)


def relay_kernel(after_ref, partner_ref, low_ref, high_ref):
    row = lax.axis_index("row")

    @pl.when((row == 1) | (row == 2))
    def _():
        for p in range(low_ref.shape[0]):
            low_ref[p], high_ref[p] = halves(partner_ref[2 * p], partner_ref[2 * p + 1])


def early_kernel(asked_ref, middle_ref, out_ref):
    row = lax.axis_index("row")

    @pl.when((row == 1) | (row == 2))
    def _():
        pick(asked_ref, 0, middle_ref, out_ref, out_ref.at[CAP // 2 :])


def late_kernel(asked_ref, passed_ref, after_ref, out_ref):
    row = lax.axis_index("row")
    half = passed_ref.shape[-1] // 2

    def side(place):
        slot = asked_ref[1, place]
        both = passed_ref[slot // 2]
        return jnp.where(slot % 2 == 0, both, turned(both))[:, :half]

    @pl.when((row == 1) | (row == 2))
    def _():
        for p in range(CAP // 2):
            out_ref[p] = jnp.concatenate([side(2 * p), side(2 * p + 1)], axis=1)


def choose_kernel(ends_ref, middles_ref, after_ref, *out_refs):
    row = lax.axis_index("row")
    for is_end, piece_ref in ((True, ends_ref), (False, middles_ref)):

        @pl.when(((row == 0) | (row == 3)) == is_end)
        def _():
            for i, out_ref in enumerate(out_refs):
                count = out_ref.shape[0]
                out_ref[...] = piece_ref[i * count : (i + 1) * count]


def fill(panel_ref, piece_refs):
    at = 0
    for piece_ref in piece_refs:
        count = piece_ref.shape[0]
        panel_ref[at : at + count] = piece_ref[...]
        at += count
    return at


def turned(block):
    half = block.shape[-1] // 2
    return jnp.concatenate([block[:, half:], block[:, :half]], axis=1)


def fetch(plan_ref, lists_ref, semaphore):
    copy = pltpu.make_async_copy(plan_ref, lists_ref, semaphore)
    copy.start()
    return copy


def room_of(lists_ref):
    return lists_ref.shape[0] // 4 - LANES // 4


def add_products(lists_ref, which, left_ref, right_ref, sum_ref, start=0):
    room = room_of(lists_ref)

    def step(c, carry):
        for p in range(CHUNK):
            first = lists_ref[which * room + 2 * (c * CHUNK + p)]
            second = lists_ref[which * room + 2 * (c * CHUNK + p) + 1]
            left = jnp.concatenate(
                [left_ref[word % FIELD - start] for word in (first, second)], axis=1
            )
            right = jnp.concatenate(
                [right_ref[(word // FIELD) % FIELD] for word in (first, second)], axis=0
            )
            sum_ref[first // (FIELD * FIELD)] += jnp.dot(
                left, right, preferred_element_type=jnp.float32
            )
        return carry

    count = lists_ref[4 * room + which]
    lax.fori_loop(0, (count + 2 * CHUNK - 1) // (2 * CHUNK), step, 0)


def near_kernel(lefts, plan_ref, *refs):
    left_refs, right_refs = refs[:lefts], refs[lefts:-6]
    sum_ref, left_ref, token_ref, right_ref, lists_ref, semaphore = refs[-6:]
    copy = fetch(plan_ref, lists_ref, semaphore)
    token_ref[...] = jnp.zeros(token_ref.shape, token_ref.dtype)
    at = fill(left_ref, left_refs)
    left_ref[at] = jnp.zeros(left_ref.shape[1:], left_ref.dtype)
    fill(right_ref, right_refs)
    sum_ref[...] = jnp.zeros(sum_ref.shape, sum_ref.dtype)
    copy.wait()
    add_products(lists_ref, 0, left_ref, right_ref, sum_ref)


def unpack(panel_ref, at, piece_ref, first, count):
    for p in range(count):
        both = piece_ref[first + p]
        panel_ref[at + 2 * p] = both
        panel_ref[at + 2 * p + 1] = turned(both)


def far_kernel(start, turn, line, plan_ref, near_ref, left_ref, after_ref, *refs):
    far_refs = refs[:-5]
    sum_ref, stored_ref, right_ref, lists_ref, semaphore = refs[-5:]
    copy = fetch(plan_ref, lists_ref, semaphore)
    right_ref[0] = jnp.zeros(right_ref.shape[1:], right_ref.dtype)
    if line:
        row = lax.axis_index("row")

        @pl.when((row == 1) | (row == 2))
        def _():
            unpack(right_ref, start, far_refs[0], 0, far_refs[0].shape[0])

        @pl.when((row == 0) | (row == 3))
        def _():
            unpack(right_ref, start, far_refs[1], turn * CAP // 2, CAP // 2)
            unpack(right_ref, start + CAP, far_refs[2], 0, CAP // 2)
    else:
        unpack(right_ref, start, far_refs[0], 0, far_refs[0].shape[0])
    for s in range(sum_ref.shape[0]):
        sum_ref[s] = turned(near_ref[s]) if turn else near_ref[s]
    copy.wait()
    add_products(lists_ref, 1, left_ref, right_ref, sum_ref)
    half = sum_ref.shape[-1] // 2
    for p in range(stored_ref.shape[0]):
        both = [sum_ref[2 * p][:, :half], sum_ref[2 * p + 1][:, :half]]
        stored_ref[p] = jnp.concatenate(both, axis=1).astype(jnp.bfloat16)


def join(panel_ref, at, low_ref, high_ref, first, second, count):
    for p in range(count):
        panel_ref[at + 2 * p], panel_ref[at + 2 * p + 1] = halves(
            low_ref[first + p], high_ref[second + p]
        )


def close_kernel(closes, nears, line, blank, plan_ref, after_ref, *refs):
    refs, (sum_ref, right_ref, token_ref, left_ref, lists_ref, semaphore) = refs[:-6], refs[-6:]
    copy = fetch(plan_ref, lists_ref, semaphore)
    sums, refs = refs[:2], refs[2:]
    lows, highs, refs = refs[:closes], refs[closes : 2 * closes], refs[2 * closes :]
    near_refs, refs = refs[:nears], refs[nears:]
    token_ref[...] = jnp.zeros(token_ref.shape, token_ref.dtype)
    at = 0
    for low_ref, high_ref in zip(lows, highs):
        join(left_ref, at, low_ref, high_ref, 0, 0, low_ref.shape[0])
        at += 2 * low_ref.shape[0]
    left_ref[blank] = jnp.zeros(left_ref.shape[1:], left_ref.dtype)
    at = fill(right_ref, near_refs)
    if line:
        passed_low_ref, passed_high_ref, early_ref, late_low_ref, late_high_ref = refs
        row = lax.axis_index("row")

        @pl.when((row == 1) | (row == 2))
        def _():
            join(right_ref, at, passed_low_ref, passed_high_ref, 0, 0, passed_low_ref.shape[0])

        @pl.when((row == 0) | (row == 3))
        def _():
            join(right_ref, at, early_ref, early_ref, 0, CAP // 2, CAP // 2)
            join(right_ref, at + CAP, late_low_ref, late_high_ref, 0, 0, CAP // 2)
    else:
        join(right_ref, at, refs[0], refs[1], 0, 0, refs[0].shape[0])
    half = sum_ref.shape[-1] // 2
    for s in range(sum_ref.shape[0]):
        both = [sums[0][s][:, :half], sums[1][s][:, :half]]
        sum_ref[s] = -1.5 * jnp.concatenate(both, axis=1)
    copy.wait()
    add_products(lists_ref, 2, left_ref, right_ref, sum_ref)


def distant_kernel(distants, start, plan_ref, close_ref, right_ref, *refs):
    lows, highs = refs[:distants], refs[distants : 2 * distants]
    out_ref, left_ref, sum_ref, lists_ref, semaphore = refs[-5:]
    copy = fetch(plan_ref, lists_ref, semaphore)
    at = 0
    for low_ref, high_ref in zip(lows, highs):
        join(left_ref, at, low_ref, high_ref, 0, 0, low_ref.shape[0])
        at += 2 * low_ref.shape[0]
    left_ref[at] = jnp.zeros(left_ref.shape[1:], left_ref.dtype)
    sum_ref[...] = close_ref[...]
    copy.wait()
    add_products(lists_ref, 3, left_ref, right_ref, sum_ref, start)
    out_ref[...] = (-2.0 * sum_ref[...]).astype(jnp.bfloat16)


def nothing_kernel(value_ref, after_ref, out_ref):
    pass


def after(value, earlier, us=0):
    return pl.pallas_call(
        nothing_kernel,
        out_shape=jax.ShapeDtypeStruct(value.shape, value.dtype),
        in_specs=[VMEM, VMEM],
        out_specs=VMEM,
        input_output_aliases={0: 0},
        compiler_params=params(8 * MIB),
        cost_estimate=cost(us),
    )(value, earlier)


def row_panel(blocks, cols, earlier=None):
    if not is_power(cols):
        return [lax.all_gather(blocks, "col", axis=0, tiled=True)]
    pieces = spread(blocks, cols // 2, cols)
    if cols > 1:
        piece = cross(blocks, cols)
        if earlier is not None:
            piece = after(piece, earlier)
        pieces += spread(piece, cols // 2, cols)
    return pieces


def cross(blocks, cols):
    return lax.ppermute(blocks, "col", [(i, i ^ (cols // 2)) for i in range(cols)])


def per_device(blocks, pairs, term_count):
    extent = blocks.shape[-1]
    slots, terms = pairs.shape[2], pairs.shape[3]
    rows, cols = lax.axis_size("row"), lax.axis_size("col")
    line = rows == 4 and cols > 1 and is_power(cols)
    local = blocks.reshape(slots, extent, extent)
    pairing = jnp.swapaxes(pairs.reshape(slots, terms, 2), 1, 2)

    def call(kernel, outs, ins, scratch=(), smem=0, out_smem=False, us=2, plan=None):
        if plan is not None:
            ins = [plan, *ins]
            scratch = [*scratch, pltpu.SMEM(plan.shape, plan.dtype), pltpu.SemaphoreType.DMA]
        first = smem if plan is None else 1
        sizes = [(a.shape, a.dtype) for a in ins[first:]]
        sizes += [(a.shape, a.dtype) for a in (scratch if plan is None else scratch[:-2])]
        sizes += [] if out_smem else outs
        vmem = 4 * MIB + sum(math.prod(shape) * jnp.dtype(dtype).itemsize for shape, dtype in sizes)
        return pl.pallas_call(
            kernel,
            out_shape=[jax.ShapeDtypeStruct(shape, dtype) for shape, dtype in outs],
            in_specs=([SMEM] * smem if plan is None else [ANY]) + [VMEM] * (len(ins) - first),
            out_specs=[SMEM if out_smem else VMEM] * len(outs),
            scratch_shapes=list(scratch),
            compiler_params=params(vmem),
            cost_estimate=cost(us),
        )(*ins)

    def blocks_of(count):
        return ((count, extent, extent), local.dtype)

    whole = ((slots, extent, extent), jnp.float32)
    requests = ((2 if line else rows, LANES), jnp.int32)
    table, request = call(
        functools.partial(prepare_kernel, slots, rows, cols, line),
        [((slots, terms), jnp.int32), requests],
        [pairing],
    )
    paired = is_power(cols) and cols > 1
    close = cols // 2 * slots if paired else cols * slots
    blank = cols * slots
    near_count = 3 * slots if line else slots
    far_count = 2 * CAP if line else rows * CAP
    right_count = near_count + far_count
    room = slots * terms + 4 * CHUNK
    plan, planned = call(
        functools.partial(plan_kernel, near_count, close, blank),
        [((4 * room + LANES,), jnp.int32), ((4,), jnp.int32)],
        [table, term_count.reshape(1, slots)],
        smem=2,
        out_smem=True,
    )
    if line:
        outer = [(i, i ^ 1) for i in range(rows)]
        inner = [(1, 2), (2, 1)]
        partner = lax.ppermute(local, "row", outer)
        ends = [row * cols + col for row in (0, 3) for col in range(cols)]
        middles = [row * cols + col for row in (1, 2) for col in range(cols)]
        other = [(i, i ^ (cols // 2)) for i in ends + middles]
        middle = lax.ppermute(
            local,
            ("row", "col"),
            [pair for pair in other if pair[0] in ends]
            + [(i, 3 * cols + i % cols - i // cols * cols) for i in middles],
        )
        crossing = lax.ppermute(
            local, ("row", "col"), [pair for pair in other if pair[0] in middles]
        )
        asked = lax.ppermute(request, "row", outer)
        halved = call(relay_kernel, [blocks_of(slots // 2)] * 2, [planned, partner], smem=1)
        passed = [lax.ppermute(piece, "row", inner) for piece in halved]
        (early,) = call(early_kernel, [blocks_of(CAP)], [asked, middle], smem=1)
        early = lax.ppermute(early, "row", outer)
        nears = [local, partner, middle]
        crossing = call(choose_kernel, [blocks_of(slots // 2)] * 2, [middle, crossing, halved[0]])
        token = halved[0]
    else:
        asked = lax.all_to_all(request, "row", split_axis=0, concat_axis=0, tiled=True)
        picked = call(pick_far_kernel, [blocks_of(rows * CAP // 2)] * 2, [asked, local], smem=1)
        token = picked[0]
        nears = [local]
        fars = [
            [lax.all_to_all(piece, "row", split_axis=0, concat_axis=0, tiled=True)]
            for piece in picked
        ]
        far_panel = [fars[0][0], fars[1][0]]
    if line:
        lefts = spread(local, cols // 2, cols)
        for pieces in zip(*(spread(piece, cols // 2, cols) for piece in crossing)):
            lefts += pieces
    else:
        lefts = row_panel(local, cols)

    def panel(count):
        return pltpu.VMEM((count, extent, extent), local.dtype)

    near, left_panel, near_token = call(
        functools.partial(near_kernel, len(lefts)),
        [whole, blocks_of(blank + 1), ((8, LANES), jnp.float32)],
        [*lefts, *nears],
        [panel(near_count)],
        plan=plan,
        us=0,
    )
    sums, squares, crossed, lates = [], [], [], []
    for turn in range(2):
        if line:
            (late,) = call(late_kernel, [blocks_of(CAP // 2)], [asked, passed[turn], token], smem=1)
            token = near_token
            lates.append(lax.ppermute(late, "row", outer))
            far = [passed[turn], early, lates[turn]]
        else:
            far = fars[turn]
        total_half, stored = call(
            functools.partial(far_kernel, near_count, turn, line),
            [whole, blocks_of(slots // 2)],
            [near, left_panel, (squares or [near])[-1], *far],
            [panel(right_count)],
            plan=plan,
        )
        sums.append(total_half)
        squares.append(stored)
        if paired:
            crossed.append(cross(stored, cols))
    if line:
        far_panel = [*passed, early, *lates]
    if paired:
        closes = [spread(stored, cols // 2, cols) for stored in squares]
    else:
        closes = [row_panel(stored, cols) for stored in squares]
        crossed = squares
    if paired:
        crossed[0] = after(crossed[0], token, 0.3)
    part, right_panel, token = call(
        functools.partial(close_kernel, len(closes[0]), len(nears), line, blank),
        [whole, blocks_of(right_count), ((8, LANES), jnp.float32)],
        [crossed[0], *sums, *closes[0], *closes[1], *nears, *far_panel],
        [panel(blank + 1)],
        plan=plan,
        us=0,
    )
    distants = [[], []]
    if paired:
        crossed[1] = after(crossed[1], token)
        distants = [spread(piece, cols // 2, cols) for piece in crossed]
    (purified,) = call(
        functools.partial(distant_kernel, len(distants[0]), close),
        [((slots, extent, extent), local.dtype)],
        [part, right_panel, *distants[0], *distants[1]],
        [panel(blank + 1 - close), pltpu.VMEM(*whole)],
        plan=plan,
    )
    return purified.reshape(blocks.shape)


def spread(blocks, extent, cols):
    pieces = {0: blocks}
    bit = extent // 2
    while bit:
        for k in list(pieces):
            pieces[k ^ bit] = lax.ppermute(pieces[k], "col", [(i, i ^ bit) for i in range(cols)])
        bit //= 2
    return [pieces[k] for k in sorted(pieces)]


def solution(mesh):
    placed = (
        P(("sys", "row"), "col", None, None, None),
        P(("sys", "row"), "col", None, None, None),
        P(("sys", "row"), "col", None),
    )
    return jax.shard_map(
        per_device,
        mesh=mesh,
        in_specs=placed,
        out_specs=P(("sys", "row"), "col", None, None, None),
        check_vma=False,
    )
```

```python
import functools
import math

import jax
import jax.numpy as jnp
from jax import lax
from jax.experimental import pallas as pl
from jax.experimental.pallas import tpu as pltpu
from jax.sharding import PartitionSpec as P

CAP = 8
LANES = 128
MIB = 1 << 20
CHUNK = 16
FIELD = 1024
SMEM = pl.BlockSpec(memory_space=pltpu.SMEM)
VMEM = pl.BlockSpec(memory_space=pltpu.VMEM)
ANY = pl.BlockSpec(memory_space=pl.ANY)


def params(limit):
    return pltpu.CompilerParams(vmem_limit_bytes=limit)


def cost(us):
    return pl.CostEstimate(
        flops=int(us * 10**9) + 10**5, bytes_accessed=int(us * 3 * 10**6) + 10**3, transcendentals=0
    )


def is_power(extent):
    return extent & (extent - 1) == 0


def prepare_kernel(slots, rows, cols, line, pairs_ref, table_ref, request_ref):
    terms = pairs_ref.shape[2]
    row, col = lax.axis_index("row"), lax.axis_index("col")
    keys = rows * slots
    key = lax.broadcasted_iota(jnp.int32, (keys, terms), 0)
    used = jnp.zeros((keys, terms), jnp.int32)
    for s in range(slots):
        used = jnp.where(pairs_ref[s, 1:2, :] == key, 1, used)
    used = jnp.max(used, axis=1, keepdims=True)
    across = lax.broadcasted_iota(jnp.int32, (keys, keys), 1)
    down = lax.broadcasted_iota(jnp.int32, (keys, keys), 0)
    before = (across // slots == down // slots) & (across < down)
    used = jnp.broadcast_to(used, (keys, LANES))
    rank = jnp.dot(
        before.astype(jnp.bfloat16),
        used.astype(jnp.bfloat16),
        preferred_element_type=jnp.float32,
    ).astype(jnp.int32)
    lane = lax.broadcasted_iota(jnp.int32, (keys, LANES), 1)
    place = lax.broadcasted_iota(jnp.int32, (keys, LANES), 0)
    listed = jnp.where((used > 0) & (rank == lane), place % slots, 0)
    source, slot, rank = key // slots, key % slots, rank[:, :terms]
    if line:
        far = jnp.abs(place // slots - row)
        for distance in (2, 3):
            part = jnp.where(far == distance, listed, 0)
            request_ref[distance - 2 : distance - 1, :] = jnp.sum(part, axis=0, keepdims=True)
        away = jnp.abs(source - row)
        is_end = (row == 0) | (row == rows - 1)
        place = jnp.where(away == 0, slot, 2 * slots + slot)
        place = jnp.where(source == row ^ 1, slots + slot, place)
        place = jnp.where(away == 2, 3 * slots + jnp.where(is_end, rank, slot), place)
        place = jnp.where(away == 3, 3 * slots + CAP + rank, place)
    else:
        request_ref[...] = jnp.sum(listed.reshape(rows, slots, LANES), axis=1)
        place = jnp.where(source == row, slot, slots + source * CAP + rank)
    for s in range(slots):
        left = pairs_ref[s, 0:1, :]
        if is_power(cols):
            left = ((left // slots) ^ col) * slots + left % slots
        hit = pairs_ref[s, 1:2, :] == key
        right = jnp.sum(jnp.where(hit, place, 0), axis=0, keepdims=True)
        table_ref[s : s + 1, :] = left + FIELD * (right + FIELD * s)


def plan_kernel(near, close, blank, table_ref, count_ref, plan_ref, token_ref):
    slots = table_ref.shape[0]
    room = plan_ref.shape[0] // 4 - LANES // 4
    token_ref[0] = 0

    def blank_of(s):
        return blank + FIELD * FIELD * s

    def block(s, ends):
        def term(t, ends):
            word = table_ref[s, t]
            is_near = ((word // FIELD) % FIELD < near).astype(jnp.int32)
            is_close = (word % FIELD < close).astype(jnp.int32)
            for end in ends:
                plan_ref[end] = word
            a, b, c, d = ends
            return a + is_near, b + 1 - is_near, c + is_close, d + 1 - is_close

        ends = lax.fori_loop(0, count_ref[0, s], term, ends)
        for end in ends:
            plan_ref[end] = blank_of(s)
        return tuple(end + end % 2 for end in ends)

    ends = lax.fori_loop(0, slots, block, tuple(jnp.int32(i * room) for i in range(4)))
    for i, end in enumerate(ends):
        plan_ref[4 * room + i] = end - i * room

        def pad(j, carry, end=end):
            plan_ref[end + j] = blank
            return carry

        lax.fori_loop(0, 2 * CHUNK, pad, 0)


def halves(first, second):
    half = first.shape[-1] // 2
    return (
        jnp.concatenate([first[:, :half], second[:, :half]], axis=1),
        jnp.concatenate([first[:, half:], second[:, half:]], axis=1),
    )


def pick(asked_ref, group, source_ref, left_ref, right_ref):
    for p in range(CAP // 2):
        first = source_ref[asked_ref[group, 2 * p]]
        second = source_ref[asked_ref[group, 2 * p + 1]]
        at = group * (CAP // 2) + p
        left_ref[at], right_ref[at] = halves(first, second)


def pick_far_kernel(asked_ref, blocks_ref, left_ref, right_ref):
    for group in range(asked_ref.shape[0]):
        pick(asked_ref, group, blocks_ref, left_ref, right_ref)


def relay_kernel(after_ref, partner_ref, low_ref, high_ref):
    row = lax.axis_index("row")

    @pl.when((row == 1) | (row == 2))
    def _():
        for p in range(low_ref.shape[0]):
            low_ref[p], high_ref[p] = halves(partner_ref[2 * p], partner_ref[2 * p + 1])


def early_kernel(asked_ref, middle_ref, out_ref):
    row = lax.axis_index("row")

    @pl.when((row == 1) | (row == 2))
    def _():
        pick(asked_ref, 0, middle_ref, out_ref, out_ref.at[CAP // 2 :])


def late_kernel(asked_ref, passed_ref, after_ref, out_ref):
    row = lax.axis_index("row")
    half = passed_ref.shape[-1] // 2

    def side(place):
        slot = asked_ref[1, place]
        both = passed_ref[slot // 2]
        return jnp.where(slot % 2 == 0, both, turned(both))[:, :half]

    @pl.when((row == 1) | (row == 2))
    def _():
        for p in range(CAP // 2):
            out_ref[p] = jnp.concatenate([side(2 * p), side(2 * p + 1)], axis=1)


def choose_kernel(ends_ref, middles_ref, after_ref, *out_refs):
    row = lax.axis_index("row")
    for is_end, piece_ref in ((True, ends_ref), (False, middles_ref)):

        @pl.when(((row == 0) | (row == 3)) == is_end)
        def _():
            for i, out_ref in enumerate(out_refs):
                count = out_ref.shape[0]
                out_ref[...] = piece_ref[i * count : (i + 1) * count]


def fill(panel_ref, piece_refs):
    at = 0
    for piece_ref in piece_refs:
        count = piece_ref.shape[0]
        panel_ref[at : at + count] = piece_ref[...]
        at += count
    return at


def turned(block):
    half = block.shape[-1] // 2
    return jnp.concatenate([block[:, half:], block[:, :half]], axis=1)


def fetch(plan_ref, lists_ref, semaphore):
    copy = pltpu.make_async_copy(plan_ref, lists_ref, semaphore)
    copy.start()
    return copy


def room_of(lists_ref):
    return lists_ref.shape[0] // 4 - LANES // 4


def add_products(lists_ref, which, left_ref, right_ref, sum_ref, start=0):
    room = room_of(lists_ref)

    def steps(pairs, at, count):
        def step(c, carry):
            for p in range(pairs):
                entry = which * room + at + 2 * (c * pairs + p)
                first, second = lists_ref[entry], lists_ref[entry + 1]
                left = jnp.concatenate(
                    [left_ref[word % FIELD - start] for word in (first, second)], axis=1
                )
                right = jnp.concatenate(
                    [right_ref[(word // FIELD) % FIELD] for word in (first, second)], axis=0
                )
                sum_ref[first // (FIELD * FIELD)] += jnp.dot(
                    left, right, preferred_element_type=jnp.float32
                )
            return carry

        lax.fori_loop(0, count, step, 0)

    count = lists_ref[4 * room + which]
    long_steps = count // (4 * CHUNK)
    steps(2 * CHUNK, 0, long_steps)
    done = long_steps * 4 * CHUNK
    steps(CHUNK, done, (count - done + 2 * CHUNK - 1) // (2 * CHUNK))


def near_kernel(lefts, plan_ref, *refs):
    left_refs, right_refs = refs[:lefts], refs[lefts:-6]
    sum_ref, left_ref, token_ref, right_ref, lists_ref, semaphore = refs[-6:]
    copy = fetch(plan_ref, lists_ref, semaphore)
    token_ref[...] = jnp.zeros(token_ref.shape, token_ref.dtype)
    at = fill(left_ref, left_refs)
    left_ref[at] = jnp.zeros(left_ref.shape[1:], left_ref.dtype)
    fill(right_ref, right_refs)
    sum_ref[...] = jnp.zeros(sum_ref.shape, sum_ref.dtype)
    copy.wait()
    add_products(lists_ref, 0, left_ref, right_ref, sum_ref)


def unpack(panel_ref, at, piece_ref, first, count):
    for p in range(count):
        both = piece_ref[first + p]
        panel_ref[at + 2 * p] = both
        panel_ref[at + 2 * p + 1] = turned(both)


def far_kernel(start, turn, line, plan_ref, near_ref, left_ref, after_ref, *refs):
    far_refs = refs[:-5]
    sum_ref, stored_ref, right_ref, lists_ref, semaphore = refs[-5:]
    copy = fetch(plan_ref, lists_ref, semaphore)
    right_ref[0] = jnp.zeros(right_ref.shape[1:], right_ref.dtype)
    if line:
        row = lax.axis_index("row")

        @pl.when((row == 1) | (row == 2))
        def _():
            unpack(right_ref, start, far_refs[0], 0, far_refs[0].shape[0])

        @pl.when((row == 0) | (row == 3))
        def _():
            unpack(right_ref, start, far_refs[1], turn * CAP // 2, CAP // 2)
            unpack(right_ref, start + CAP, far_refs[2], 0, CAP // 2)
    else:
        unpack(right_ref, start, far_refs[0], 0, far_refs[0].shape[0])
    for s in range(sum_ref.shape[0]):
        sum_ref[s] = turned(near_ref[s]) if turn else near_ref[s]
    copy.wait()
    add_products(lists_ref, 1, left_ref, right_ref, sum_ref)
    half = sum_ref.shape[-1] // 2
    for p in range(stored_ref.shape[0]):
        both = [sum_ref[2 * p][:, :half], sum_ref[2 * p + 1][:, :half]]
        stored_ref[p] = jnp.concatenate(both, axis=1).astype(jnp.bfloat16)


def join(panel_ref, at, low_ref, high_ref, first, second, count):
    for p in range(count):
        panel_ref[at + 2 * p], panel_ref[at + 2 * p + 1] = halves(
            low_ref[first + p], high_ref[second + p]
        )


def close_kernel(closes, nears, line, blank, plan_ref, after_ref, *refs):
    refs, (sum_ref, right_ref, token_ref, left_ref, lists_ref, semaphore) = refs[:-6], refs[-6:]
    copy = fetch(plan_ref, lists_ref, semaphore)
    sums, refs = refs[:2], refs[2:]
    lows, highs, refs = refs[:closes], refs[closes : 2 * closes], refs[2 * closes :]
    near_refs, refs = refs[:nears], refs[nears:]
    token_ref[...] = jnp.zeros(token_ref.shape, token_ref.dtype)
    at = 0
    for low_ref, high_ref in zip(lows, highs):
        join(left_ref, at, low_ref, high_ref, 0, 0, low_ref.shape[0])
        at += 2 * low_ref.shape[0]
    left_ref[blank] = jnp.zeros(left_ref.shape[1:], left_ref.dtype)
    at = fill(right_ref, near_refs)
    if line:
        passed_low_ref, passed_high_ref, early_ref, late_low_ref, late_high_ref = refs
        row = lax.axis_index("row")

        @pl.when((row == 1) | (row == 2))
        def _():
            join(right_ref, at, passed_low_ref, passed_high_ref, 0, 0, passed_low_ref.shape[0])

        @pl.when((row == 0) | (row == 3))
        def _():
            join(right_ref, at, early_ref, early_ref, 0, CAP // 2, CAP // 2)
            join(right_ref, at + CAP, late_low_ref, late_high_ref, 0, 0, CAP // 2)
    else:
        join(right_ref, at, refs[0], refs[1], 0, 0, refs[0].shape[0])
    half = sum_ref.shape[-1] // 2
    for s in range(sum_ref.shape[0]):
        both = [sums[0][s][:, :half], sums[1][s][:, :half]]
        sum_ref[s] = -1.5 * jnp.concatenate(both, axis=1)
    copy.wait()
    add_products(lists_ref, 2, left_ref, right_ref, sum_ref)


def distant_kernel(distants, start, plan_ref, close_ref, right_ref, *refs):
    lows, highs = refs[:distants], refs[distants : 2 * distants]
    out_ref, left_ref, sum_ref, lists_ref, semaphore = refs[-5:]
    copy = fetch(plan_ref, lists_ref, semaphore)
    at = 0
    for low_ref, high_ref in zip(lows, highs):
        join(left_ref, at, low_ref, high_ref, 0, 0, low_ref.shape[0])
        at += 2 * low_ref.shape[0]
    left_ref[at] = jnp.zeros(left_ref.shape[1:], left_ref.dtype)
    sum_ref[...] = close_ref[...]
    copy.wait()
    add_products(lists_ref, 3, left_ref, right_ref, sum_ref, start)
    out_ref[...] = (-2.0 * sum_ref[...]).astype(jnp.bfloat16)


def nothing_kernel(value_ref, after_ref, out_ref):
    pass


def after(value, earlier, us=0):
    return pl.pallas_call(
        nothing_kernel,
        out_shape=jax.ShapeDtypeStruct(value.shape, value.dtype),
        in_specs=[VMEM, VMEM],
        out_specs=VMEM,
        input_output_aliases={0: 0},
        compiler_params=params(8 * MIB),
        cost_estimate=cost(us),
    )(value, earlier)


def row_panel(blocks, cols, earlier=None):
    if not is_power(cols):
        return [lax.all_gather(blocks, "col", axis=0, tiled=True)]
    pieces = spread(blocks, cols // 2, cols)
    if cols > 1:
        piece = cross(blocks, cols)
        if earlier is not None:
            piece = after(piece, earlier)
        pieces += spread(piece, cols // 2, cols)
    return pieces


def cross(blocks, cols):
    return lax.ppermute(blocks, "col", [(i, i ^ (cols // 2)) for i in range(cols)])


def per_device(blocks, pairs, term_count):
    extent = blocks.shape[-1]
    slots, terms = pairs.shape[2], pairs.shape[3]
    rows, cols = lax.axis_size("row"), lax.axis_size("col")
    line = rows == 4 and cols > 1 and is_power(cols)
    local = blocks.reshape(slots, extent, extent)
    pairing = jnp.swapaxes(pairs.reshape(slots, terms, 2), 1, 2)

    def call(kernel, outs, ins, scratch=(), smem=0, out_smem=False, us=2, plan=None):
        if plan is not None:
            ins = [plan, *ins]
            scratch = [*scratch, pltpu.SMEM(plan.shape, plan.dtype), pltpu.SemaphoreType.DMA]
        first = smem if plan is None else 1
        sizes = [(a.shape, a.dtype) for a in ins[first:]]
        sizes += [(a.shape, a.dtype) for a in (scratch if plan is None else scratch[:-2])]
        sizes += [] if out_smem else outs
        vmem = 4 * MIB + sum(math.prod(shape) * jnp.dtype(dtype).itemsize for shape, dtype in sizes)
        return pl.pallas_call(
            kernel,
            out_shape=[jax.ShapeDtypeStruct(shape, dtype) for shape, dtype in outs],
            in_specs=([SMEM] * smem if plan is None else [ANY]) + [VMEM] * (len(ins) - first),
            out_specs=[SMEM if out_smem else VMEM] * len(outs),
            scratch_shapes=list(scratch),
            compiler_params=params(vmem),
            cost_estimate=cost(us),
        )(*ins)

    def blocks_of(count):
        return ((count, extent, extent), local.dtype)

    whole = ((slots, extent, extent), jnp.float32)
    requests = ((2 if line else rows, LANES), jnp.int32)
    table, request = call(
        functools.partial(prepare_kernel, slots, rows, cols, line),
        [((slots, terms), jnp.int32), requests],
        [pairing],
    )
    paired = is_power(cols) and cols > 1
    close = cols // 2 * slots if paired else cols * slots
    blank = cols * slots
    near_count = 3 * slots if line else slots
    far_count = 2 * CAP if line else rows * CAP
    right_count = near_count + far_count
    room = slots * terms + 4 * CHUNK
    plan, planned = call(
        functools.partial(plan_kernel, near_count, close, blank),
        [((4 * room + LANES,), jnp.int32), ((4,), jnp.int32)],
        [table, term_count.reshape(1, slots)],
        smem=2,
        out_smem=True,
    )
    if line:
        outer = [(i, i ^ 1) for i in range(rows)]
        inner = [(1, 2), (2, 1)]
        partner = lax.ppermute(local, "row", outer)
        ends = [row * cols + col for row in (0, 3) for col in range(cols)]
        middles = [row * cols + col for row in (1, 2) for col in range(cols)]
        other = [(i, i ^ (cols // 2)) for i in ends + middles]
        middle = lax.ppermute(
            local,
            ("row", "col"),
            [pair for pair in other if pair[0] in ends]
            + [(i, 3 * cols + i % cols - i // cols * cols) for i in middles],
        )
        crossing = lax.ppermute(
            local, ("row", "col"), [pair for pair in other if pair[0] in middles]
        )
        asked = lax.ppermute(request, "row", outer)
        halved = call(relay_kernel, [blocks_of(slots // 2)] * 2, [planned, partner], smem=1)
        (early,) = call(early_kernel, [blocks_of(CAP)], [asked, middle], smem=1)
        passed = [
            lax.ppermute(piece, "row", inner) for piece in (halved[0], after(halved[1], early))
        ]
        early = lax.ppermute(early, "row", outer)
        nears = [local, partner, middle]
        crossing = call(choose_kernel, [blocks_of(slots // 2)] * 2, [middle, crossing, halved[0]])
        token = halved[0]
    else:
        asked = lax.all_to_all(request, "row", split_axis=0, concat_axis=0, tiled=True)
        picked = call(pick_far_kernel, [blocks_of(rows * CAP // 2)] * 2, [asked, local], smem=1)
        token = picked[0]
        nears = [local]
        fars = [
            [lax.all_to_all(piece, "row", split_axis=0, concat_axis=0, tiled=True)]
            for piece in picked
        ]
        far_panel = [fars[0][0], fars[1][0]]
    if line:
        lefts = spread(local, cols // 2, cols)
        for pieces in zip(*(spread(piece, cols // 2, cols) for piece in crossing)):
            lefts += pieces
    else:
        lefts = row_panel(local, cols)

    def panel(count):
        return pltpu.VMEM((count, extent, extent), local.dtype)

    near, left_panel, near_token = call(
        functools.partial(near_kernel, len(lefts)),
        [whole, blocks_of(blank + 1), ((8, LANES), jnp.float32)],
        [*lefts, *nears],
        [panel(near_count)],
        plan=plan,
        us=0,
    )
    sums, squares, crossed, lates = [], [], [], []
    for turn in range(2):
        if line:
            (late,) = call(late_kernel, [blocks_of(CAP // 2)], [asked, passed[turn], token], smem=1)
            token = near_token
            lates.append(lax.ppermute(late, "row", outer))
            far = [passed[turn], early, lates[turn]]
        else:
            far = fars[turn]
        total_half, stored = call(
            functools.partial(far_kernel, near_count, turn, line),
            [whole, blocks_of(slots // 2)],
            [near, left_panel, (squares or [near])[-1], *far],
            [panel(right_count)],
            plan=plan,
        )
        sums.append(total_half)
        squares.append(stored)
        if paired:
            crossed.append(cross(stored, cols))
    if line:
        far_panel = [*passed, early, *lates]
    if paired:
        closes = [spread(stored, cols // 2, cols) for stored in squares]
    else:
        closes = [row_panel(stored, cols) for stored in squares]
        crossed = squares
    if paired:
        crossed[0] = after(crossed[0], token, 0.3)
    part, right_panel, token = call(
        functools.partial(close_kernel, len(closes[0]), len(nears), line, blank),
        [whole, blocks_of(right_count), ((8, LANES), jnp.float32)],
        [crossed[0], *sums, *closes[0], *closes[1], *nears, *far_panel],
        [panel(blank + 1)],
        plan=plan,
        us=0,
    )
    distants = [[], []]
    if paired:
        crossed[1] = after(crossed[1], token)
        distants = [spread(piece, cols // 2, cols) for piece in crossed]
    (purified,) = call(
        functools.partial(distant_kernel, len(distants[0]), close),
        [((slots, extent, extent), local.dtype)],
        [part, right_panel, *distants[0], *distants[1]],
        [panel(blank + 1 - close), pltpu.VMEM(*whole)],
        plan=plan,
    )
    return purified.reshape(blocks.shape)


def spread(blocks, extent, cols):
    pieces = {0: blocks}
    bit = extent // 2
    while bit:
        for k in list(pieces):
            pieces[k ^ bit] = lax.ppermute(pieces[k], "col", [(i, i ^ bit) for i in range(cols)])
        bit //= 2
    return [pieces[k] for k in sorted(pieces)]


def solution(mesh):
    placed = (
        P(("sys", "row"), "col", None, None, None),
        P(("sys", "row"), "col", None, None, None),
        P(("sys", "row"), "col", None),
    )
    return jax.shard_map(
        per_device,
        mesh=mesh,
        in_specs=placed,
        out_specs=P(("sys", "row"), "col", None, None, None),
        check_vma=False,
    )
```
